32 devices in a mesh: dp: 8 (over y, x, core), seq: 4 (over z).
Axes of the slice: x: 2, y: 2, z: 4, core: 2. Of those that a mesh axis runs over, the one named last changes fastest.
Arguments:
- inputs: bfloat16 [32, 1024, 1024], P('dp', 'seq'), may hold values from -6 to 6
- doc_ids: int32 [32, 1024], P('dp'), may hold values from 0 to 4, as said below
- cotangent: bfloat16 [32, 1024, 1024], P('dp', 'seq'), may hold values from -6 to 6
- norm_gains: float32 [2, 1024], P(None, ('dp', 'seq')), may hold values from 0.2 to 2
- gains_first: float32 [2, 1024], P(None, ('dp', 'seq')), may hold values from -0.0008544922 to 0.0008544922
- gains_second: float32 [2, 1024], P(None, ('dp', 'seq')), may hold values from 1.6348702e-08 to 6.403242e-08
- kernel: float32 [3, 1024], P(None, ('dp', 'seq')), may hold values from -3.5 to 3.5
- kernel_first: float32 [3, 1024], P(None, ('dp', 'seq')), may hold values from -0.00061035156 to 0.00061035156
- kernel_second: float32 [3, 1024], P(None, ('dp', 'seq')), may hold values from 7.220677e-09 to 2.8610229e-08
- w_in: float32 [1024, 3072], P(('dp', 'seq')), may hold values from -0.1875 to 0.1875
- w_in_first: float32 [1024, 3072], P(('dp', 'seq')), may hold values from -0.00061035156 to 0.00061035156
- w_in_second: float32 [1024, 3072], P(('dp', 'seq')), may hold values from 7.220677e-09 to 2.8610229e-08
- w_out: float32 [1024, 1024], P(('dp', 'seq')), may hold values from -0.1875 to 0.1875
- w_out_first: float32 [1024, 1024], P(('dp', 'seq')), may hold values from -0.00061035156 to 0.00061035156
- w_out_second: float32 [1024, 1024], P(('dp', 'seq')), may hold values from 7.220677e-09 to 2.8610229e-08
- w_gate: float32 [1024, 4608], P(('dp', 'seq')), may hold values from -0.1875 to 0.1875
- w_gate_first: float32 [1024, 4608], P(('dp', 'seq')), may hold values from -0.00030517578 to 0.00030517578
- w_gate_second: float32 [1024, 4608], P(('dp', 'seq')), may hold values from 1.7711095e-09 to 7.220677e-09
- w_up: float32 [1024, 4608], P(('dp', 'seq')), may hold values from -0.1875 to 0.1875
- w_up_first: float32 [1024, 4608], P(('dp', 'seq')), may hold values from -0.00030517578 to 0.00030517578
- w_up_second: float32 [1024, 4608], P(('dp', 'seq')), may hold values from 1.7711095e-09 to 7.220677e-09
- w_down: float32 [4608, 1024], P(('dp', 'seq')), may hold values from -0.09375 to 0.09375
- w_down_first: float32 [4608, 1024], P(('dp', 'seq')), may hold values from -0.00030517578 to 0.00030517578
- w_down_second: float32 [4608, 1024], P(('dp', 'seq')), may hold values from 1.7711095e-09 to 7.220677e-09
Outputs:
- block_out: bfloat16 [32, 1024, 1024], P('dp', 'seq')
- input_grad: float32 [32, 1024, 1024], P('dp', 'seq')
- grad_norm: float32 [], replicated
- gains_first_new: float32 [2, 1024], P(None, ('dp', 'seq'))
- gains_second_new: float32 [2, 1024], P(None, ('dp', 'seq'))
- gains_new: float32 [2, 1024], P(None, ('dp', 'seq'))
- kernel_first_new: float32 [3, 1024], P(None, ('dp', 'seq'))
- updated_tap_variance: float32 [3, 1024], P(None, ('dp', 'seq'))
- kernel_new: float32 [3, 1024], P(None, ('dp', 'seq'))
- w_in_first_new: float32 [1024, 3072], P(('dp', 'seq'))
- w_in_second_new: float32 [1024, 3072], P(('dp', 'seq'))
- w_in_new: float32 [1024, 3072], P(('dp', 'seq'))
- w_out_first_new: float32 [1024, 1024], P(('dp', 'seq'))
- w_out_second_new: float32 [1024, 1024], P(('dp', 'seq'))
- w_out_new: float32 [1024, 1024], P(('dp', 'seq'))
- w_gate_first_new: float32 [1024, 4608], P(('dp', 'seq'))
- w_gate_second_new: float32 [1024, 4608], P(('dp', 'seq'))
- w_gate_new: float32 [1024, 4608], P(('dp', 'seq'))
- w_up_first_new: float32 [1024, 4608], P(('dp', 'seq'))
- w_up_second_new: float32 [1024, 4608], P(('dp', 'seq'))
- w_up_new: float32 [1024, 4608], P(('dp', 'seq'))
- w_down_first_new: float32 [4608, 1024], P(('dp', 'seq'))
- w_down_second_new: float32 [4608, 1024], P(('dp', 'seq'))
- w_down_new: float32 [4608, 1024], P(('dp', 'seq'))
The draws below stay inside these ranges and needn't reach their ends.
Inputs may be any that keep to these rules, and one draw needn't show every extreme that they name: `doc_ids`: each sequence holds exactly five documents: numbers start at 0 at its first token and rise by one at each document's first token; tokens with equal numbers belong to one document.
All inputs are finite; a program needn't handle non-finite values.
Results may differ from the reference program's by a relative error of at most 0.012.
The reference program's roundings to bfloat16 on the way count: a program that leaves them out, or rounds other values in their place, can miss the bound.
Values may be sent and summed in bfloat16 or wider, within the bound.
A program may use at most 320 MiB of HBM per device.

```python
import math
import jax
import jax.numpy as jnp
from jax import lax

D = 1024
FF = 4608
LEN = 1024
STEP = 10
SEQ_ALL = 32


def draw_doc_ids(key, part):
    key = jax.random.fold_in(key, 11)
    key_start = jax.random.fold_in(key, 1)
    key_end = jax.random.fold_in(key, 2)
    key_head = jax.random.fold_in(key, 3)
    key_tail = jax.random.fold_in(key, 4)
    quarter = LEN // 4
    opening = jax.random.randint(key_start, (SEQ_ALL, 1), 3, quarter)
    closing = jax.random.randint(key_end, (SEQ_ALL, 1), 3 * quarter + 1, LEN - 2)
    head_mark = jax.random.randint(key_head, (SEQ_ALL, 1), 1, opening)
    tail_mark = jax.random.randint(key_tail, (SEQ_ALL, 1), closing + 1, LEN)
    places = jnp.arange(LEN, dtype=jnp.int32)[None, :]
    starts = (places == head_mark) | (places == opening) | (places == closing) | (places == tail_mark)
    return jnp.cumsum(starts.astype(jnp.int32), axis=1).astype(jnp.int32)


def draw_norm_gains(key, part):
    key = jax.random.fold_in(key, 5)
    ramp = jnp.arange(D, dtype=jnp.float32) / D
    noise = jax.random.uniform(key, (2, D), jnp.float32, -1.0, 1.0)
    base = 0.5 + ramp
    return base[None, :] * (1.0 + 0.3 * noise)


def levels(key, dims, cuts, low, top_value):
    def one(position, blocks):
        heights = jax.random.uniform(jax.random.fold_in(jax.random.fold_in(key, 6), position), (blocks,), jnp.float32, low / len(cuts), top_value / len(cuts))
        return jnp.repeat(jnp.exp(heights), dims[position] // blocks).reshape((-1,) + (1,) * (len(dims) - position - 1))

    level = one(*cuts[0])
    for cut in cuts[1:]:
        level = level * one(*cut)
    return level


def centred(key, extent, scale, most, cuts=(), kind=jnp.bfloat16):
    drawn = scale * jax.random.normal(key, extent, jnp.float32)
    if cuts:
        drawn = drawn * levels(key, extent, cuts, -0.22, 0.18)
    return jnp.clip(drawn, -most, most).astype(kind)


def setup_inputs(seed: int = 0) -> dict:
    key_of = jax.random.split(jax.random.key(seed), 25)
    inputs = centred(key_of[0], (SEQ_ALL, LEN, D), 1.0, 6.0, ((0, 8), (1, 4)))
    doc_ids = draw_doc_ids(jax.random.fold_in(key_of[24], 71), 0)
    cotangent = centred(key_of[2], (SEQ_ALL, LEN, D), 1.0, 6.0, ((0, 8), (1, 4)))
    norm_gains = draw_norm_gains(jax.random.fold_in(key_of[24], 71), 0)
    gains_first = centred(key_of[4], (2, D), (0.16 * (4 * D * D + 2 * D * FF // 3) ** -0.5), 0.0008544922, ((1, 32),), jnp.float32)
    gains_second = jnp.clip(jnp.exp(math.log(6.403242025498912e-08) - 1.365241 * jax.random.uniform(key_of[5], (2, D), jnp.float32) ** levels(key_of[5], (2, D), ((1, 32),), -0.2, 0.2)), 1.6348701947777045e-08, 6.403242025498912e-08)
    kernel = centred(key_of[6], (3, D), 3 ** -0.5, 3.5, ((1, 32),), jnp.float32)
    kernel_first = centred(key_of[7], (3, D), (0.11 * (4 * D * D + 2 * D * FF // 3) ** -0.5), 0.00061035156, ((1, 32),), jnp.float32)
    kernel_second = jnp.clip(jnp.exp(math.log(2.8610228852699038e-08) - 1.3768156 * jax.random.uniform(key_of[8], (3, D), jnp.float32) ** levels(key_of[8], (3, D), ((1, 32),), -0.2, 0.2)), 7.22067694525208e-09, 2.8610228852699038e-08)
    w_in = centred(key_of[9], (D, 3 * D), D ** -0.5, 0.1875, ((0, 32),), jnp.float32)
    w_in_first = centred(key_of[10], (D, 3 * D), (0.11 * (4 * D * D + 2 * D * FF // 3) ** -0.5), 0.00061035156, ((0, 32),), jnp.float32)
    w_in_second = jnp.clip(jnp.exp(math.log(2.8610228852699038e-08) - 1.3768156 * jax.random.uniform(key_of[11], (D, 3 * D), jnp.float32) ** levels(key_of[11], (D, 3 * D), ((0, 32),), -0.2, 0.2)), 7.22067694525208e-09, 2.8610228852699038e-08)
    w_out = centred(key_of[12], (D, D), D ** -0.5, 0.1875, ((0, 32),), jnp.float32)
    w_out_first = centred(key_of[13], (D, D), (0.11 * (4 * D * D + 2 * D * FF // 3) ** -0.5), 0.00061035156, ((0, 32),), jnp.float32)
    w_out_second = jnp.clip(jnp.exp(math.log(2.8610228852699038e-08) - 1.3768156 * jax.random.uniform(key_of[14], (D, D), jnp.float32) ** levels(key_of[14], (D, D), ((0, 32),), -0.2, 0.2)), 7.22067694525208e-09, 2.8610228852699038e-08)
    w_gate = centred(key_of[15], (D, FF), D ** -0.5, 0.1875, ((0, 32),), jnp.float32)
    w_gate_first = centred(key_of[16], (D, FF), (0.055 * (4 * D * D + 2 * D * FF // 3) ** -0.5), 0.00030517578, ((0, 32),), jnp.float32)
    w_gate_second = jnp.clip(jnp.exp(math.log(7.22067694525208e-09) - 1.40534253 * jax.random.uniform(key_of[17], (D, FF), jnp.float32) ** levels(key_of[17], (D, FF), ((0, 32),), -0.2, 0.2)), 1.7711094812966621e-09, 7.22067694525208e-09)
    w_up = centred(key_of[18], (D, FF), D ** -0.5, 0.1875, ((0, 32),), jnp.float32)
    w_up_first = centred(key_of[19], (D, FF), (0.055 * (4 * D * D + 2 * D * FF // 3) ** -0.5), 0.00030517578, ((0, 32),), jnp.float32)
    w_up_second = jnp.clip(jnp.exp(math.log(7.22067694525208e-09) - 1.40534253 * jax.random.uniform(key_of[20], (D, FF), jnp.float32) ** levels(key_of[20], (D, FF), ((0, 32),), -0.2, 0.2)), 1.7711094812966621e-09, 7.22067694525208e-09)
    w_down = centred(key_of[21], (FF, D), FF ** -0.5, 0.09375, ((0, 32),), jnp.float32)
    w_down_first = centred(key_of[22], (FF, D), (0.055 * (4 * D * D + 2 * D * FF // 3) ** -0.5), 0.00030517578, ((0, 32),), jnp.float32)
    w_down_second = jnp.clip(jnp.exp(math.log(7.22067694525208e-09) - 1.40534253 * jax.random.uniform(key_of[23], (FF, D), jnp.float32) ** levels(key_of[23], (FF, D), ((0, 32),), -0.2, 0.2)), 1.7711094812966621e-09, 7.22067694525208e-09)
    return dict(inputs=inputs, doc_ids=doc_ids, cotangent=cotangent, norm_gains=norm_gains, gains_first=gains_first, gains_second=gains_second, kernel=kernel, kernel_first=kernel_first, kernel_second=kernel_second, w_in=w_in, w_in_first=w_in_first, w_in_second=w_in_second, w_out=w_out, w_out_first=w_out_first, w_out_second=w_out_second, w_gate=w_gate, w_gate_first=w_gate_first, w_gate_second=w_gate_second, w_up=w_up, w_up_first=w_up_first, w_up_second=w_up_second, w_down=w_down, w_down_first=w_down_first, w_down_second=w_down_second)


EPS_NORM = 1e-05
BETA_ONE = 0.9
BETA_TWO = 0.95
ADAM_EPS = 1e-08
DECAY = 0.1
RATE = 2.0
CLIP = 1.0
HIGH = lax.Precision.HIGHEST

@jax.custom_vjp
def low(v):
    return lax.optimization_barrier(v.astype(jnp.bfloat16)).astype(jnp.float32)

@jax.custom_vjp
def low_back(v):
    return v

def low_keep(v):
    return (low(v), None)

def low_pass(kept, grad):
    return (grad,)

def back_keep(v):
    return (v, None)

def back_low(kept, grad):
    return (low(grad),)
low.defvjp(low_keep, low_pass)
low_back.defvjp(back_keep, back_low)

def rms_scale(values, gain):
    return values * lax.rsqrt(lax.optimization_barrier(jnp.mean(values * values, axis=-1, keepdims=True)) + EPS_NORM) * gain

def causal_conv(values, taps, block_ids):
    length = values.shape[1]
    result = values * taps[2]
    for lag in (1, 2):
        shifted = jnp.pad(values, ((0, 0), (lag, 0), (0, 0)))[:, :length]
        earlier = jnp.pad(block_ids, ((0, 0), (lag, 0)), constant_values=-1)[:, :length]
        shared_document_mask = (earlier == block_ids).astype(jnp.float32)[..., None]
        result = result + shifted * shared_document_mask * taps[2 - lag]
    return result

def forward(weights, values, block_ids):
    gain_pair, taps, w_in, w_out, w_gate, w_up, w_down = weights
    gain_pair = low(gain_pair)
    taps = low(taps)
    w_in = low(w_in)
    w_out = low(w_out)
    w_gate = low(w_gate)
    w_up = low(w_up)
    w_down = low(w_down)
    width = w_out.shape[0]
    rescaled_source = low(rms_scale(values, gain_pair[0]))
    mixed_columns = low_back(jnp.einsum('gld,de->gle', rescaled_source, w_in, precision=HIGH))
    part_b = mixed_columns[..., :width]
    part_c = mixed_columns[..., width:2 * width]
    part_x = mixed_columns[..., 2 * width:]
    gated = low(part_b * part_x)
    conv_out = low_back(causal_conv(gated, taps, block_ids))
    branch_values = low(part_c * conv_out)
    hidden_one = values + low_back(jnp.einsum('gld,de->gle', branch_values, w_out, precision=HIGH))
    second_normed_input = low(rms_scale(hidden_one, gain_pair[1]))
    gate_preactivation = low_back(jnp.einsum('gld,df->glf', second_normed_input, w_gate, precision=HIGH))
    up_preactivation = low_back(jnp.einsum('gld,df->glf', second_normed_input, w_up, precision=HIGH))
    activated_hidden = low(jax.nn.silu(gate_preactivation) * up_preactivation)
    return hidden_one + low_back(jnp.einsum('glf,fd->gld', activated_hidden, w_down, precision=HIGH))

def adam_update(master, first, second, gradient, factor, rate):
    clipped = gradient * factor
    new_first = BETA_ONE * first + (1.0 - BETA_ONE) * clipped
    new_second = BETA_TWO * second + (1.0 - BETA_TWO) * clipped * clipped
    first_hat = new_first / (1.0 - BETA_ONE ** STEP)
    second_hat = new_second / (1.0 - BETA_TWO ** STEP)
    new_master = master - rate * (first_hat / (jnp.sqrt(second_hat) + ADAM_EPS) + DECAY * master)
    return (new_first, new_second, new_master)

def reference(inputs, doc_ids, cotangent, norm_gains, gains_first, gains_second, kernel, kernel_first, kernel_second, w_in, w_in_first, w_in_second, w_out, w_out_first, w_out_second, w_gate, w_gate_first, w_gate_second, w_up, w_up_first, w_up_second, w_down, w_down_first, w_down_second):
    params = (norm_gains, kernel, w_in, w_out, w_gate, w_up, w_down)
    seq_total = inputs.shape[0]
    group_size = math.gcd(seq_total, max(1, 4096 // LEN))
    groups_count = seq_total // group_size
    stacked_in = inputs.astype(jnp.float32).reshape(groups_count, group_size, LEN, D)
    stacked_ids = doc_ids.reshape(groups_count, group_size, LEN)
    stacked_cot = cotangent.astype(jnp.float32).reshape(groups_count, group_size, LEN, D)

    def one_group(running, pieces):
        block_in, block_ids, block_cot = pieces

        def apply_block(weights, values):
            return forward(weights, values, block_ids)
        result, pullback = jax.vjp(apply_block, params, block_in)
        weight_grads, input_weight_gradient = pullback(block_cot)
        running = tuple((preceding_token + addend for preceding_token, addend in zip(running, weight_grads)))
        return (running, (result.astype(jnp.bfloat16), input_weight_gradient))
    zero_grads = tuple((jnp.zeros_like(weight) for weight in params))
    gradients, (outputs, in_grads) = lax.scan(one_group, zero_grads, (stacked_in, stacked_ids, stacked_cot))
    squares = jnp.float32(0.0)
    for gradient in gradients:
        squares = squares + jnp.sum(gradient * gradient)
    grad_norm = jnp.sqrt(squares)
    factor = CLIP / jnp.maximum(grad_norm, CLIP)
    matrix_rate = RATE / math.sqrt(D)
    gains_first_new, gains_second_new, gains_new = adam_update(norm_gains, gains_first, gains_second, gradients[0], factor, RATE * 0.3)
    kernel_first_new, updated_tap_variance, kernel_new = adam_update(kernel, kernel_first, kernel_second, gradients[1], factor, RATE * 0.6)
    w_in_first_new, w_in_second_new, w_in_new = adam_update(w_in, w_in_first, w_in_second, gradients[2], factor, matrix_rate)
    w_out_first_new, w_out_second_new, w_out_new = adam_update(w_out, w_out_first, w_out_second, gradients[3], factor, matrix_rate)
    w_gate_first_new, w_gate_second_new, w_gate_new = adam_update(w_gate, w_gate_first, w_gate_second, gradients[4], factor, matrix_rate)
    w_up_first_new, w_up_second_new, w_up_new = adam_update(w_up, w_up_first, w_up_second, gradients[5], factor, matrix_rate)
    w_down_first_new, w_down_second_new, w_down_new = adam_update(w_down, w_down_first, w_down_second, gradients[6], factor, RATE / math.sqrt(FF))
    block_out = outputs.reshape(seq_total, LEN, D)
    input_grad = in_grads.reshape(seq_total, LEN, D)
    return (block_out, input_grad, grad_norm, gains_first_new, gains_second_new, gains_new, kernel_first_new, updated_tap_variance, kernel_new, w_in_first_new, w_in_second_new, w_in_new, w_out_first_new, w_out_second_new, w_out_new, w_gate_first_new, w_gate_second_new, w_gate_new, w_up_first_new, w_up_second_new, w_up_new, w_down_first_new, w_down_second_new, w_down_new)
```

```python
import math

import jax
import jax.numpy as jnp
from jax import lax
from jax.sharding import PartitionSpec as P

D = 1024
FF = 4608
STEP = 10


EPS_NORM = 1e-05
BETA_ONE = 0.9
BETA_TWO = 0.95
ADAM_EPS = 1e-08
DECAY = 0.1
RATE = 2.0
CLIP = 1.0


def from_behind(shard, axis, by):
    devices = lax.axis_size(axis)
    pairs = [(i, i + by) for i in range(devices) if 0 <= i + by < devices]
    return lax.ppermute(shard, axis, pairs)


def bits_of(size):
    return size.bit_length() - 1


def swap_bit(shard, bit):
    devices = lax.axis_size("dp")
    return lax.ppermute(shard, "dp", [(i, i ^ (1 << bit)) for i in range(devices)])


def swap_seq(shard, by):
    devices = lax.axis_size("seq")
    return lax.ppermute(shard, "seq", [(i, (i + by) % devices) for i in range(devices)])


def bit_order(flipped):
    order = list(range(1, bits_of(lax.axis_size("dp"))))
    return order[::-1] if flipped else order


def collect(shard, flipped):
    span = lax.axis_size("seq")
    place = lax.axis_index("seq")
    row = lax.axis_index("dp")
    arrived = jnp.stack([shard] + [swap_seq(shard, by) for by in range(1, span)])
    held = jnp.stack(
        [
            lax.dynamic_index_in_dim(arrived, (place - i + span) % span, 0, keepdims=False)
            for i in range(span)
        ]
    )
    seen = []
    for bit in bit_order(flipped) + [0]:
        other = swap_bit(held, bit)
        upper = ((row >> bit) & 1) == 1
        axis = sum(1 for b in seen if b > bit)
        held = jnp.stack(
            [jnp.where(upper, other, held), jnp.where(upper, held, other)], axis=axis
        )
        seen.append(bit)
    return held


def gather_rows(shard, flipped):
    full = collect(shard.astype(jnp.bfloat16), flipped)
    return full.reshape((-1, full.shape[-1]))


def scatter_sum(parts, flipped):
    span = lax.axis_size("seq")
    place = lax.axis_index("seq")
    row = lax.axis_index("dp")
    kind = parts.dtype
    left = list(range(bits_of(lax.axis_size("dp"))))
    for bit in [0] + bit_order(flipped)[::-1]:
        axis = sum(1 for b in left if b > bit)
        mine = (row >> bit) & 1
        away = lax.dynamic_index_in_dim(parts, 1 - mine, axis, keepdims=False)
        kept = lax.dynamic_index_in_dim(parts, mine, axis, keepdims=False)
        came = swap_bit(away, bit)
        parts = (kept.astype(jnp.float32) + came.astype(jnp.float32)).astype(kind)
        left.remove(bit)
    total = lax.dynamic_index_in_dim(parts, place, 0, keepdims=False).astype(jnp.float32)
    for by in range(1, span):
        away = lax.dynamic_index_in_dim(parts, (place + by) % span, 0, keepdims=False)
        total = total + swap_seq(away, by).astype(jnp.float32)
    return total


def scatter_rows(gradient, flipped):
    span = lax.axis_size("seq")
    bits = bits_of(lax.axis_size("dp"))
    rows = gradient.shape[0] // ((1 << bits) * span)
    parts = gradient.astype(jnp.bfloat16).reshape((2,) * bits + (span, rows, gradient.shape[1]))
    return scatter_sum(parts, flipped)


def sum_everywhere(value):
    tile = jnp.full((8, 128), value, jnp.float32)
    for axis in ("seq", "dp"):
        devices = lax.axis_size(axis)
        step = 1
        while step < devices:
            radix = 4 if step * 4 <= devices else 2
            terms = [tile] + [
                lax.ppermute(tile, axis, [(i, i ^ (k * step)) for i in range(devices)])
                for k in range(1, radix)
            ]
            while len(terms) > 1:
                terms = [terms[i] + terms[i + 1] for i in range(0, len(terms), 2)]
            tile = terms[0]
            step *= radix
    return tile[0, 0]


def adam_update(master, first, second, gradient, factor, rate):
    clipped = gradient * factor
    new_first = BETA_ONE * first + (1.0 - BETA_ONE) * clipped
    new_second = BETA_TWO * second + (1.0 - BETA_TWO) * clipped * clipped
    first_hat = new_first / (1.0 - BETA_ONE**STEP)
    second_hat = new_second / (1.0 - BETA_TWO**STEP)
    new_master = master - rate * (first_hat / (jnp.sqrt(second_hat) + ADAM_EPS) + DECAY * master)
    return (new_first, new_second, new_master)


def local(
    inputs,
    doc_ids,
    cotangent,
    norm_gains,
    gains_first,
    gains_second,
    kernel,
    kernel_first,
    kernel_second,
    w_in,
    w_in_first,
    w_in_second,
    w_out,
    w_out_first,
    w_out_second,
    w_gate,
    w_gate_first,
    w_gate_second,
    w_up,
    w_up_first,
    w_up_second,
    w_down,
    w_down_first,
    w_down_second,
):
    low_small = jnp.concatenate([norm_gains, kernel], axis=0).astype(jnp.bfloat16)
    small = collect(low_small, False)
    small = small.reshape((-1,) + low_small.shape).transpose(1, 0, 2).reshape(low_small.shape[0], -1)
    full_gains = small[:2]
    full_kernel = small[2:]
    collected_entry_matrix = gather_rows(w_in, False)
    gathered_output_weight = gather_rows(w_out, True)
    gathered_gate_weight = gather_rows(w_gate, False)
    gathered_up_weight = gather_rows(w_up, True)
    gathered_down_weight = gather_rows(w_down, True)
    gain_wide = full_gains.astype(jnp.float32)
    taps = full_kernel.astype(jnp.float32)
    width = inputs.shape[2]
    span = inputs.shape[1]
    position = lax.axis_index("seq") * span
    padded_ids = jnp.pad(doc_ids, ((0, 0), (2, 2)), constant_values=-1)
    near_ids = lax.dynamic_slice_in_dim(padded_ids, position, span + 4, 1)
    centre = near_ids[:, 2 : span + 2]
    same_one = (near_ids[:, 1 : span + 1] == centre).astype(jnp.float32)[..., None]
    matching_lag_pair = (near_ids[:, :span] == centre).astype(jnp.float32)[..., None]
    next_one = (near_ids[:, 3 : span + 3] == centre).astype(jnp.float32)[..., None]
    next_two = (near_ids[:, 4 : span + 4] == centre).astype(jnp.float32)[..., None]
    values = inputs.astype(jnp.float32)
    scale_one = lax.rsqrt(jnp.mean(values * values, axis=-1, keepdims=True) + EPS_NORM)
    rescaled_source = (values * scale_one * gain_wide[0]).astype(jnp.bfloat16)
    mixed_columns = jnp.einsum(
        "uwt,tf->uwf", rescaled_source, collected_entry_matrix, preferred_element_type=jnp.float32
    )
    part_b = mixed_columns[..., :width]
    part_c = mixed_columns[..., width : 2 * width]
    part_x = mixed_columns[..., 2 * width :]
    gated = (part_b * part_x).astype(jnp.bfloat16)
    upper_rim = from_behind(gated[:, span - 2 :], "seq", 1)
    extended = jnp.concatenate([upper_rim, gated], axis=1).astype(jnp.float32)
    lag_one = extended[:, 1 : span + 1] * same_one
    lag_two = extended[:, :span] * matching_lag_pair
    current = extended[:, 2:]
    conv_out = current * taps[2] + lag_one * taps[1] + lag_two * taps[0]
    branch_values = (part_c * conv_out).astype(jnp.bfloat16)
    hidden_one = values + jnp.einsum(
        "uwt,tf->uwf", branch_values, gathered_output_weight, preferred_element_type=jnp.float32
    )
    scale_two = lax.rsqrt(jnp.mean(hidden_one * hidden_one, axis=-1, keepdims=True) + EPS_NORM)
    second_normed_input = (hidden_one * scale_two * gain_wide[1]).astype(jnp.bfloat16)
    gate_preactivation = jnp.einsum(
        "wyz,zm->wym", second_normed_input, gathered_gate_weight, preferred_element_type=jnp.float32
    )
    up_preactivation = jnp.einsum(
        "wyz,zm->wym", second_normed_input, gathered_up_weight, preferred_element_type=jnp.float32
    )
    sigma = jax.nn.sigmoid(gate_preactivation)
    silu_val = gate_preactivation * sigma
    activated_hidden = (silu_val * up_preactivation).astype(jnp.bfloat16)
    block_out = (
        hidden_one
        + jnp.einsum(
            "vyk,kx->vyx",
            activated_hidden,
            gathered_down_weight,
            preferred_element_type=jnp.float32,
        )
    ).astype(jnp.bfloat16)
    activated_gradient = jnp.einsum(
        "uar,tr->uat", cotangent, gathered_down_weight, preferred_element_type=jnp.float32
    )
    down_weight_gradient = jnp.einsum(
        "vna,vnw->aw", activated_hidden, cotangent, preferred_element_type=jnp.float32
    )
    gate_input_gradient = (
        activated_gradient * up_preactivation * sigma * (1.0 + gate_preactivation * (1.0 - sigma))
    ).astype(jnp.bfloat16)
    up_input_gradient = (activated_gradient * silu_val).astype(jnp.bfloat16)
    second_normed_gradient = jnp.einsum(
        "npg,kg->npk", gate_input_gradient, gathered_gate_weight, preferred_element_type=jnp.float32
    )
    second_normed_gradient = second_normed_gradient + jnp.einsum(
        "npg,kg->npk", up_input_gradient, gathered_up_weight, preferred_element_type=jnp.float32
    )
    gate_weight_gradient = jnp.einsum(
        "rbz,rbx->zx", second_normed_input, gate_input_gradient, preferred_element_type=jnp.float32
    )
    up_weight_gradient = jnp.einsum(
        "rbz,rbx->zx", second_normed_input, up_input_gradient, preferred_element_type=jnp.float32
    )
    gain_two_grad = jnp.sum(second_normed_gradient * hidden_one * scale_two, axis=(0, 1))
    zeta_two = second_normed_gradient * gain_wide[1]
    d_hidden = (
        cotangent.astype(jnp.float32)
        + scale_two * zeta_two
        - hidden_one * scale_two**3 * jnp.mean(zeta_two * hidden_one, axis=-1, keepdims=True)
    )
    branch_output_gradient = d_hidden.astype(jnp.bfloat16)
    branch_gradient = jnp.einsum(
        "fxh,dh->fxd",
        branch_output_gradient,
        gathered_output_weight,
        preferred_element_type=jnp.float32,
    )
    output_weight_gradient = jnp.einsum(
        "ncr,ncj->rj", branch_values, branch_output_gradient, preferred_element_type=jnp.float32
    )
    d_part_c = branch_gradient * conv_out
    d_conv = (branch_gradient * part_c).astype(jnp.bfloat16)
    lower_rim = from_behind(d_conv[:, :2], "seq", -1)
    conv_ext = jnp.concatenate([d_conv, lower_rim], axis=1).astype(jnp.float32)
    d_conv_own = conv_ext[:, :span]
    d_gated = (
        d_conv_own * taps[2]
        + conv_ext[:, 1 : span + 1] * next_one * taps[1]
        + conv_ext[:, 2:] * next_two * taps[0]
    )
    kernel_grad = jnp.stack(
        [
            jnp.sum(d_conv_own * lag_two, axis=(0, 1)),
            jnp.sum(d_conv_own * lag_one, axis=(0, 1)),
            jnp.sum(d_conv_own * current, axis=(0, 1)),
        ]
    )
    convolved_derivative = jnp.concatenate(
        [d_gated * part_x, d_part_c, d_gated * part_b], axis=-1
    ).astype(jnp.bfloat16)
    normed_gradient = jnp.einsum(
        "fxh,dh->fxd",
        convolved_derivative,
        collected_entry_matrix,
        preferred_element_type=jnp.float32,
    )
    input_weight_gradient = jnp.einsum(
        "ncr,ncj->rj", rescaled_source, convolved_derivative, preferred_element_type=jnp.float32
    )
    first_scale_derivative = jnp.sum(normed_gradient * values * scale_one, axis=(0, 1))
    zeta_one = normed_gradient * gain_wide[0]
    input_grad = (
        d_hidden
        + scale_one * zeta_one
        - values * scale_one**3 * jnp.mean(zeta_one * values, axis=-1, keepdims=True)
    )
    small_grads = jnp.concatenate(
        [first_scale_derivative[None], gain_two_grad[None], kernel_grad], axis=0
    )
    columns = norm_gains.shape[1]
    parts = small_grads.reshape(small_grads.shape[0], -1, columns).transpose(1, 0, 2)
    parts = parts.reshape(
        (2,) * bits_of(lax.axis_size("dp"))
        + (lax.axis_size("seq"), small_grads.shape[0], columns)
    )
    small_shard = scatter_sum(parts, False)
    shards = (
        small_shard[:2],
        small_shard[2:],
        scatter_rows(input_weight_gradient, False),
        scatter_rows(output_weight_gradient, True),
        scatter_rows(gate_weight_gradient, False),
        scatter_rows(up_weight_gradient, True),
        scatter_rows(down_weight_gradient, True),
    )
    squares = jnp.float32(0.0)
    for portion in shards:
        squares = squares + jnp.sum(portion * portion)
    grad_norm = jnp.sqrt(sum_everywhere(squares))
    factor = CLIP / jnp.maximum(grad_norm, CLIP)
    matrix_rate = RATE / math.sqrt(D)
    gains_first_new, gains_second_new, gains_new = adam_update(
        norm_gains, gains_first, gains_second, shards[0], factor, RATE * 0.3
    )
    kernel_first_new, updated_tap_variance, kernel_new = adam_update(
        kernel, kernel_first, kernel_second, shards[1], factor, RATE * 0.6
    )
    w_in_first_new, w_in_second_new, w_in_new = adam_update(
        w_in, w_in_first, w_in_second, shards[2], factor, matrix_rate
    )
    w_out_first_new, w_out_second_new, w_out_new = adam_update(
        w_out, w_out_first, w_out_second, shards[3], factor, matrix_rate
    )
    w_gate_first_new, w_gate_second_new, w_gate_new = adam_update(
        w_gate, w_gate_first, w_gate_second, shards[4], factor, matrix_rate
    )
    w_up_first_new, w_up_second_new, w_up_new = adam_update(
        w_up, w_up_first, w_up_second, shards[5], factor, matrix_rate
    )
    w_down_first_new, w_down_second_new, w_down_new = adam_update(
        w_down, w_down_first, w_down_second, shards[6], factor, RATE / math.sqrt(FF)
    )
    return (
        block_out,
        input_grad,
        grad_norm,
        gains_first_new,
        gains_second_new,
        gains_new,
        kernel_first_new,
        updated_tap_variance,
        kernel_new,
        w_in_first_new,
        w_in_second_new,
        w_in_new,
        w_out_first_new,
        w_out_second_new,
        w_out_new,
        w_gate_first_new,
        w_gate_second_new,
        w_gate_new,
        w_up_first_new,
        w_up_second_new,
        w_up_new,
        w_down_first_new,
        w_down_second_new,
        w_down_new,
    )


def solution(mesh):
    return jax.shard_map(
        local,
        mesh=mesh,
        in_specs=(
            P("dp", "seq", None),
            P("dp", None),
            P("dp", "seq", None),
            P(None, ("dp", "seq")),
            P(None, ("dp", "seq")),
            P(None, ("dp", "seq")),
            P(None, ("dp", "seq")),
            P(None, ("dp", "seq")),
            P(None, ("dp", "seq")),
            P(("dp", "seq"), None),
            P(("dp", "seq"), None),
            P(("dp", "seq"), None),
            P(("dp", "seq"), None),
            P(("dp", "seq"), None),
            P(("dp", "seq"), None),
            P(("dp", "seq"), None),
            P(("dp", "seq"), None),
            P(("dp", "seq"), None),
            P(("dp", "seq"), None),
            P(("dp", "seq"), None),
            P(("dp", "seq"), None),
            P(("dp", "seq"), None),
            P(("dp", "seq"), None),
            P(("dp", "seq"), None),
        ),
        out_specs=(
            P("dp", "seq", None),
            P("dp", "seq", None),
            P(),
            P(None, ("dp", "seq")),
            P(None, ("dp", "seq")),
            P(None, ("dp", "seq")),
            P(None, ("dp", "seq")),
            P(None, ("dp", "seq")),
            P(None, ("dp", "seq")),
            P(("dp", "seq"), None),
            P(("dp", "seq"), None),
            P(("dp", "seq"), None),
            P(("dp", "seq"), None),
            P(("dp", "seq"), None),
            P(("dp", "seq"), None),
            P(("dp", "seq"), None),
            P(("dp", "seq"), None),
            P(("dp", "seq"), None),
            P(("dp", "seq"), None),
            P(("dp", "seq"), None),
            P(("dp", "seq"), None),
            P(("dp", "seq"), None),
            P(("dp", "seq"), None),
            P(("dp", "seq"), None),
        ),
        check_vma=False,
    )
```
